32 devices in a mesh: shot: 8 (over z, x), rcv: 2 (over y), surf: 2 (over core).
Axes of the slice: x: 2, y: 2, z: 4, core: 2. Of those that a mesh axis runs over, the one named last changes fastest.
Arguments:
- traces: bfloat16 [2, 8192, 256], P('surf', 'shot'), may hold values from -6 to 6
- trace_block: int32 [2, 8192, 1], P('surf', 'shot'), may hold values from 0 to 7; in each aligned block of 512 rows (0 to 511, 512 to 1023, ..., all dimensions but the last counted through in order) at most 128 rows name the same one
- trace_shot: int32 [2, 8192], P('surf', 'shot'), may hold values from 0 to 15
- trace_point: int32 [2, 8192], P('surf', 'shot'), may hold values from 0 to 255
- recv_panel: bfloat16 [129, 2, 512, 256], P(None, None, ('shot', 'surf'), 'rcv'), may hold values from -0.375 to 0.375
Outputs:
- multiples: bfloat16 [129, 2, 128, 256], P(None, None, ('shot', 'surf'), 'rcv')
The draws below stay inside these ranges and needn't reach their ends.
Inputs may be any that keep to these rules, and one draw needn't show every extreme that they name: `trace_block`: in each aligned block of 512 rows, at most 128 rows name one shot block.
All inputs are finite; a program needn't handle non-finite values.
Results may differ from the reference program's by a relative error of at most 0.012.
Values may be sent and summed in bfloat16 or wider, within the bound.
No kernel may reach another device: no remote copies, remote signals or barrier semaphores. Data moves between devices by JAX's collectives and lax.ppermute only.
A program may use at most 64 MiB of HBM per device.

```python
import math
import jax
import jax.numpy as jnp
import numpy as np
from jax import lax

WINDOW = 256
F = 129
K = 512
SHOTS_PER_INDEX = 16
RC_DEV = 128
TR_DEV = 1024
PART_ROWS = 512
CAP = 128
KD = 256
RCVS = 256
N_SHOT = 8
N_RCV = 2
N_SURF = 2


def plant(entries, own_key, smallest, top_value):
    longest = entries.shape.index(max(entries.shape))
    spots = []
    for shift in (0, 1):
        where = [jax.random.randint(jax.random.fold_in(own_key, axis), (), 0, length) for axis, length in enumerate(entries.shape)]
        where[longest] = (where[longest] + shift) % entries.shape[longest]
        spots.append(tuple(where))
    return entries.at[spots[0]].set(smallest).at[spots[1]].set(top_value)


def levels(key, extent, pieces, low, largest):
    gain = 1.0
    for dim, parts in pieces:
        draws = jax.random.uniform(jax.random.fold_in(jax.random.fold_in(key, 6), dim), (parts,), jnp.float32, low / len(pieces), largest / len(pieces))
        gain = gain * jnp.repeat(jnp.exp(draws), extent[dim] // parts).reshape((-1,) + (1,) * (len(extent) - 1 - dim))
    return gain


def deal_out(key, own, number, rows, amount, top, reach, lean):
    sequence = jax.random.permutation(key, amount)
    heavy_load, usual = shares(amount, rows * top, reach, lean, True), shares(amount, rows * top, reach, lean, False)
    places = jnp.arange(amount)

    def named(sizes, offset_by):
        used = int((sizes > 0).sum())
        fixed = max(1, used // 4)
        moved = fixed + (places - fixed + offset_by * (used - fixed)) % max(1, amount - fixed)
        return jnp.zeros((amount,), jnp.int32).at[sequence[jnp.where(places < fixed, places, moved)]].set(jnp.asarray(sizes, jnp.int32))

    sizes = jnp.where(number % 4 == 0, named(heavy_load, number // 4), named(usual, number - number // 4 - 1))
    mixed = jax.random.permutation(jax.random.fold_in(own, 3), amount)
    giver, taker = mixed[0:amount // 2 * 2:2], mixed[1:amount // 2 * 2:2]
    margin = jnp.minimum(sizes[giver] - 1, reach - sizes[taker]) // 2
    margin = jnp.where((giver == sequence[0]) | (taker == sequence[0]) | (sizes[taker] == 0), 0, jnp.maximum(margin, 0))
    moved = jax.random.randint(jax.random.fold_in(own, 4), (amount // 2,), 0, 1 << 20) % (margin + 1)
    sizes = sizes.at[giver].add(-moved).at[taker].add(moved)
    labels = jnp.searchsorted(jnp.cumsum(sizes), jnp.arange(rows * top), side="right").astype(jnp.int32)
    table = labels.reshape(top, rows).T
    table = table[jax.random.permutation(jax.random.fold_in(own, 1), rows)]
    offset_by = jax.random.randint(jax.random.fold_in(own, 2), (rows, 1), 0, top)
    return jnp.take_along_axis(table, (jnp.arange(top)[None, :] + offset_by) % top, axis=1)


def shares(amount, total, limit, skew, full):
    weights = [(1 << 20) // math.isqrt(standing ** skew) + 1 for standing in range(1, amount + 1)]
    largest = limit if full else min(limit, max(-(-total // amount), total * weights[0] // sum(weights)))
    least = 1 if total - largest >= amount - 1 else 0
    given, rest = [largest] + [least] * (amount - 1), total - largest - least * (amount - 1)
    while rest > 0:
        candidates = [i for i in range(1, amount) if given[i] < largest] or [i for i in range(1, amount) if given[i] < limit]
        pool, remaining = sum([weights[i] for i in candidates]), rest
        for i in candidates:
            more = min(limit - given[i], max(1, remaining * weights[i] // pool), rest)
            given[i] = given[i] + more
            rest = rest - more
    return np.array(given)


def gaussian(own_key, shape, deviation, bound, pieces=(), held_as=jnp.bfloat16):
    entries = deviation * jax.random.normal(own_key, shape, jnp.float32)
    if pieces:
        entries = entries * levels(own_key, shape, pieces, -0.22, 0.18)
    return jnp.clip(entries, -bound, bound).astype(held_as)


def setup_inputs(seed: int = 0) -> dict:
    key_list = jax.random.split(jax.random.key(seed), 6)
    traces = gaussian(key_list[0], (N_SURF, TR_DEV * N_SHOT, WINDOW), 1.0, 6.0, ((0, 2), (1, 8)))
    trace_block_keys = jax.random.split(jax.random.fold_in(key_list[1], 1), N_SURF * (TR_DEV * N_SHOT) // PART_ROWS)
    trace_block_turns = jax.random.permutation(jax.random.fold_in(key_list[1], 3), N_SURF * (TR_DEV * N_SHOT) // PART_ROWS)
    trace_block = jax.vmap(lambda own, number: deal_out(jax.random.fold_in(key_list[1], 2), own, number, PART_ROWS, N_SHOT, 1, CAP, 2))(trace_block_keys, trace_block_turns).reshape((N_SURF, TR_DEV * N_SHOT, 1))
    trace_shot = plant(jax.random.randint(key_list[2], (N_SURF, TR_DEV * N_SHOT), 0, SHOTS_PER_INDEX), jax.random.fold_in(key_list[2], 1), 0, SHOTS_PER_INDEX - 1).astype(jnp.int32)
    trace_point = plant(jax.random.randint(key_list[3], (N_SURF, TR_DEV * N_SHOT), 0, KD), jax.random.fold_in(key_list[3], 1), 0, KD - 1).astype(jnp.int32)
    recv_panel = gaussian(key_list[4], (F, 2, K, RCVS), (K // 2) ** -0.5, 0.375, ((2, 16), (3, 2)))
    return {"traces": traces, "trace_block": trace_block, "trace_shot": trace_shot, "trace_point": trace_point, "recv_panel": recv_panel}


def rounded(values):
    return lax.optimization_barrier(values.astype(jnp.bfloat16)).astype(jnp.float32)


def reference(traces, trace_block, trace_shot, trace_point, recv_panel):
    half_window_width = K // N_SURF
    block_width = K // (N_SHOT * N_SURF)
    shot_total = SHOTS_PER_INDEX * N_SHOT
    rcv_total = RC_DEV * N_RCV
    samples = traces.astype(jnp.float32)
    spectrum = jnp.fft.rfft(samples, axis=-1) * (WINDOW ** -0.5)
    pairs = rounded(jnp.stack([jnp.real(spectrum), jnp.imag(spectrum)], axis=2))
    half_index = lax.broadcasted_iota(jnp.int32, trace_shot.shape, 0)
    source_shot_index = trace_block[:, :, 0] * SHOTS_PER_INDEX + trace_shot
    bin_position_index = ((source_shot_index * N_SURF + half_index) * half_window_width + trace_point).reshape(-1).astype(jnp.int32)
    flat_rows = pairs.reshape(-1, 2, F)
    sums = jax.ops.segment_sum(flat_rows, bin_position_index, num_segments=shot_total * K)
    coverage = jax.ops.segment_sum(jnp.ones(bin_position_index.shape, jnp.float32), bin_position_index, num_segments=shot_total * K)
    panel = (sums / jnp.maximum(coverage, 1.0)[:, None, None]).astype(jnp.bfloat16)
    panel = panel.reshape(shot_total, N_SURF, half_window_width, 2, F).transpose(4, 1, 3, 0, 2)
    receiver = recv_panel.reshape(F, 2, N_SHOT, N_SURF, block_width, rcv_total)
    receiver = receiver.transpose(0, 3, 1, 2, 4, 5).reshape(F, N_SURF, 2, half_window_width, rcv_total)

    def one_freq(pair):
        left_edge = pair[0].astype(jnp.float32)
        right_edge = pair[1].astype(jnp.float32)

        def product(first, second):
            return jnp.einsum("hsk,hkr->hsr", first, second)

        real_part = product(left_edge[:, 0], right_edge[:, 0]) - product(left_edge[:, 1], right_edge[:, 1])
        imag_part = product(left_edge[:, 0], right_edge[:, 1]) + product(left_edge[:, 1], right_edge[:, 0])
        partial_value = rounded(jnp.stack([real_part, imag_part], axis=1))
        return jnp.sum(partial_value, axis=0).astype(jnp.bfloat16)

    return lax.map(one_freq, (panel, receiver))
```

```python
import functools
import math

import jax
import jax.numpy as jnp
import numpy as np
from jax import lax
from jax.experimental import pallas as pl
from jax.experimental.pallas import tpu as pltpu
from jax.sharding import PartitionSpec as P

SHOTS_PER_INDEX = 16
VMEM = pl.BlockSpec(memory_space=pltpu.VMEM)
SMEM = pl.BlockSpec(memory_space=pltpu.SMEM)
LIMIT = 56 * 1024 * 1024


def dft_tables(window, groups, width, top):
    slots = -(-(2 * width + 4) // 16) * 16
    n = np.arange(window, dtype=np.int64)
    table = np.zeros((groups, slots, window), np.float64)
    for g in range(groups):
        freqs = list(range(g * width, (g + 1) * width)) + [top]
        for j, f in enumerate(freqs):
            angle = (n * f % window) * (2.0 * math.pi / window)
            table[g, 2 * j] = np.cos(angle)
            table[g, 2 * j + 1] = -np.sin(angle)
    table = (table / math.sqrt(window)).astype(np.float32)
    high = table.astype(jnp.bfloat16)
    low = (table - high.astype(np.float32)).astype(jnp.bfloat16)
    return high, low, slots


def nt(a, b):
    return lax.dot_general(a, b, (((1,), (1,)), ((), ())), preferred_element_type=jnp.float32)


def spectra_kernel(slots, id_slot, x_ref, high_ref, low_ref, shot_ref, point_ref, out_ref):
    x = x_ref[...]
    y = nt(high_ref[...], x) + nt(low_ref[...], x)
    groups = out_ref.shape[0]
    y = y.reshape(groups, slots, x.shape[0])
    place = lax.broadcasted_iota(jnp.int32, y.shape, 1)
    y = jnp.where(place == id_slot, shot_ref[...].astype(jnp.float32)[None], y)
    y = jnp.where(place == id_slot + 1, point_ref[...].astype(jnp.float32)[None], y)
    out_ref[...] = y.astype(jnp.bfloat16)


def bin_kernel(
    halves, shots, points, cols, id_slot, me_ref, rows_ref, own_ref, panel_ref, top_ref, acc_ref, top_acc_ref
):
    sources = rows_ref.shape[0] // halves
    width = own_ref.shape[1]
    n_rows = rows_ref.shape[2]
    own_shot, own_half = me_ref[0], me_ref[1]

    def hits(source, count, slot, first):
        ids = rows_ref[source, slot : slot + 1, :].astype(jnp.float32) - first
        grid = lax.broadcasted_iota(jnp.int32, (count, n_rows), 0).astype(jnp.float32)
        return jnp.where(grid == ids, 1.0, 0.0).astype(jnp.bfloat16)

    for half in range(halves):

        def step(s, carry):
            source = s * halves + half
            shot_hit = hits(source, shots, id_slot, 0.0)
            point_hit = hits(source, points, id_slot + 1, 0.0)
            for c in range(cols + 1):
                left = shot_hit if c == cols else shot_hit * rows_ref[source, c : c + 1, :]
                got = nt(left, point_hit)
                acc_ref[c] = jnp.where(s == 0, got, acc_ref[c] + got)
            return carry

        lax.fori_loop(0, sources, step, 0)
        scale = 1.0 / jnp.maximum(acc_ref[cols], 1.0)
        for c in range(cols):
            panel_ref[c, :, half * points : (half + 1) * points] = (acc_ref[c] * scale).astype(jnp.bfloat16)

    def top_step(s, carry):
        source = s * halves + own_half
        shot_hit = hits(source, shots, id_slot, 0.0)
        point_hit = hits(source, width, id_slot + 1, (own_shot * width).astype(jnp.float32))
        for c in range(3):
            left = shot_hit if c == 2 else shot_hit * rows_ref[source, cols + c : cols + c + 1, :]
            got = nt(left, point_hit)
            top_acc_ref[c] = jnp.where(s == 0, got, top_acc_ref[c] + got)
        return carry

    lax.fori_loop(0, sources, top_step, 0)
    scale = 1.0 / jnp.maximum(top_acc_ref[2], 1.0)
    real = (top_acc_ref[0] * scale).astype(jnp.bfloat16)
    imag = (top_acc_ref[1] * scale).astype(jnp.bfloat16)
    dot = functools.partial(jnp.dot, preferred_element_type=jnp.float32)
    own_real, own_imag = own_ref[0], own_ref[1]
    out_real = dot(real, own_real) - dot(imag, own_imag)
    out_imag = dot(real, own_imag) + dot(imag, own_real)
    targets = top_ref.shape[0]
    block = shots // targets
    for t in range(targets):
        rows = slice(t * block, (t + 1) * block)
        top_ref[t] = jnp.concatenate([out_real[rows], out_imag[rows]], axis=0).astype(jnp.bfloat16)


def product_kernel(n_shot, n_rcv, halves, width, panel_ref, recv_ref, out_ref):
    shots = panel_ref.shape[1]
    left = panel_ref[...].reshape(2 * shots, panel_ref.shape[2])
    sides = []
    for c in range(2):
        blocks = []
        for r in range(n_rcv):
            rows = [
                recv_ref[(s * n_rcv + r) * halves + h, c * width : (c + 1) * width, :]
                for h in range(halves)
                for s in range(n_shot)
            ]
            blocks.append(jnp.concatenate(rows, axis=0))
        right = blocks[0] if n_rcv == 1 else jnp.concatenate(blocks, axis=1)
        sides.append(jnp.dot(left, right, preferred_element_type=jnp.float32))
    real = sides[0][:shots] - sides[1][shots:]
    imag = sides[1][:shots] + sides[0][shots:]
    lanes = recv_ref.shape[2]
    block = shots // (n_shot * halves)
    for s in range(n_shot):
        for h in range(halves):
            first = (s * halves + h) * block
            both = jnp.concatenate([real[first : first + block], imag[first : first + block]], axis=0)
            for r in range(n_rcv):
                out_ref[(s * n_rcv + r) * halves + h] = both[:, r * lanes : (r + 1) * lanes].astype(jnp.bfloat16)


def local(traces, trace_block, trace_shot, trace_point, recv_panel):
    n_shot, n_rcv, halves = lax.axis_size("shot"), lax.axis_size("rcv"), lax.axis_size("surf")
    freqs, _, width, lanes = recv_panel.shape
    window, n_rows = traces.shape[2], traces.shape[1]
    shots, points = SHOTS_PER_INDEX * n_shot, width * n_shot
    assert max(shots, points) <= 256
    main = freqs - 1
    pairs = n_shot * halves
    spread = main % (pairs * n_rcv) == 0
    across = n_rcv if spread else 1
    axes = ("shot", "rcv", "surf") if spread else ("shot", "surf")
    groups = pairs * across
    per = main // groups
    cols = 2 * per
    block = shots // pairs
    high, low, slots = dft_tables(window, groups, per, main)

    def own_table(table):
        table = jnp.asarray(table).reshape(n_shot, across, halves, slots, window)
        table = lax.dynamic_index_in_dim(table, lax.axis_index("rcv") if spread else 0, 1, keepdims=False)
        return table.reshape(pairs * slots, window)

    shot_ids = trace_block.reshape(1, n_rows) * SHOTS_PER_INDEX + trace_shot
    me = jnp.stack([lax.axis_index("shot"), lax.axis_index("surf")]).astype(jnp.int32)

    recv = recv_panel[:main].reshape(groups, per * 2 * width, lanes)
    recv = lax.all_to_all(recv, axes, split_axis=0, concat_axis=0, tiled=True)

    message = pl.pallas_call(
        functools.partial(spectra_kernel, slots, cols + 2),
        out_shape=jax.ShapeDtypeStruct((pairs, slots, n_rows), jnp.bfloat16),
        in_specs=[VMEM] * 5,
        out_specs=VMEM,
        compiler_params=pltpu.CompilerParams(vmem_limit_bytes=LIMIT),
    )(traces[0], own_table(high), own_table(low), shot_ids, trace_point)
    rows = lax.all_to_all(message, ("shot", "surf"), split_axis=0, concat_axis=0, tiled=True)

    panel, top = pl.pallas_call(
        functools.partial(bin_kernel, halves, shots, points, cols, cols + 2),
        out_shape=(
            jax.ShapeDtypeStruct((cols, shots, halves * points), jnp.bfloat16),
            jax.ShapeDtypeStruct((pairs, 2 * block, lanes), jnp.bfloat16),
        ),
        in_specs=[SMEM, VMEM, VMEM],
        out_specs=(VMEM, VMEM),
        scratch_shapes=[
            pltpu.VMEM((cols + 1, shots, points), jnp.float32),
            pltpu.VMEM((3, shots, width), jnp.float32),
        ],
        compiler_params=pltpu.CompilerParams(vmem_limit_bytes=LIMIT),
    )(me, rows, recv_panel[main])
    top = lax.all_to_all(top, ("shot", "surf"), split_axis=0, concat_axis=0, tiled=True)
    top = jnp.sum(top.astype(jnp.float32), axis=0).astype(jnp.bfloat16).reshape(1, 2, block, lanes)

    out = pl.pallas_call(
        functools.partial(product_kernel, n_shot, across, halves, width),
        grid=(per,),
        out_shape=jax.ShapeDtypeStruct((groups, per * 2 * block, lanes), jnp.bfloat16),
        in_specs=[
            pl.BlockSpec((2, shots, halves * points), lambda f: (f, 0, 0)),
            pl.BlockSpec((groups, 2 * width, lanes), lambda f: (0, f, 0)),
        ],
        out_specs=pl.BlockSpec((groups, 2 * block, lanes), lambda f: (0, f, 0)),
        compiler_params=pltpu.CompilerParams(vmem_limit_bytes=LIMIT),
    )(panel, recv)
    out = lax.all_to_all(out, axes, split_axis=0, concat_axis=0, tiled=True)
    return jnp.concatenate([out.reshape(main, 2, block, lanes), top], axis=0)


def solution(mesh):
    in_specs = (
        P("surf", "shot", None),
        P("surf", "shot", None),
        P("surf", "shot"),
        P("surf", "shot"),
        P(None, None, ("shot", "surf"), "rcv"),
    )
    out_specs = P(None, None, ("shot", "surf"), "rcv")
    return jax.shard_map(local, mesh=mesh, in_specs=in_specs, out_specs=out_specs, check_vma=False)
```

```python
import functools
import math

import jax
import jax.numpy as jnp
import numpy as np
from jax import lax
from jax.experimental import pallas as pl
from jax.experimental.pallas import tpu as pltpu
from jax.sharding import PartitionSpec as P

SHOTS_PER_INDEX = 16
VMEM = pl.BlockSpec(memory_space=pltpu.VMEM)
LANES = 128
LIMIT = 16 * 1024 * 1024


def dft_tables(window, outer, across, inner, per, top):
    slots = 2 * per + 4
    n = np.arange(window, dtype=np.int64)
    table = np.zeros((outer, across, inner, slots, window), np.float64)
    for o in range(outer):
        for a in range(across):
            for i in range(inner):
                first = ((o * across + a) * inner + i) * per
                for j, f in enumerate(list(range(first, first + per)) + [top]):
                    angle = (n * f % window) * (2.0 * math.pi / window)
                    table[o, a, i, 2 * j] = np.cos(angle)
                    table[o, a, i, 2 * j + 1] = -np.sin(angle)
    table = (table / math.sqrt(window)).astype(np.float32)
    table = table.transpose(1, 0, 2, 3, 4).reshape(across, outer * inner * slots, window)
    high = table.astype(jnp.bfloat16)
    low = (table - high.astype(np.float32)).astype(jnp.bfloat16)
    return jnp.asarray(high), jnp.asarray(low), slots


def nt(a, b):
    return lax.dot_general(a, b, (((1,), (1,)), ((), ())), preferred_element_type=jnp.float32)


def spectra_kernel(slots, x_ref, high_ref, low_ref, block_ref, shot_ref, point_ref, out_ref):
    x = x_ref[...]
    mine = lax.axis_index("rcv") if high_ref.shape[0] > 1 else 0
    y = nt(high_ref[mine], x) + nt(low_ref[mine], x)
    shot = (block_ref[...] * SHOTS_PER_INDEX + shot_ref[...]).astype(jnp.float32)
    point = point_ref[...].astype(jnp.float32)
    for g in range(out_ref.shape[0]):
        pieces = []
        for j in range(x.shape[0] // LANES):
            lanes = slice(j * LANES, (j + 1) * LANES)
            pieces += [y[g * slots : (g + 1) * slots - 2, lanes], shot[:, lanes], point[:, lanes]]
        out_ref[g] = jnp.concatenate(pieces, axis=0).astype(jnp.bfloat16)


def bin_kernel(halves, shots, points, cols, rows_ref, own_ref, panel_ref, top_ref, acc_ref, top_acc_ref):
    sources = rows_ref.shape[0] // halves
    width = own_ref.shape[1]
    slots = cols + 4
    parts = rows_ref.shape[1] // slots
    own_shot, own_half = lax.axis_index("shot"), lax.axis_index("surf")

    def row(source, slot):
        return [rows_ref[source, j * slots + slot : j * slots + slot + 1, :] for j in range(parts)]

    def hits(source, count, slot, first):
        grid = lax.broadcasted_iota(jnp.int32, (count, LANES), 0).astype(jnp.float32)
        return [
            jnp.where(grid == ids.astype(jnp.float32) - first, 1.0, 0.0).astype(jnp.bfloat16)
            for ids in row(source, slot)
        ]

    def summed(into_ref, s, source, shot_hit, point_hit, chosen):
        for c, slot in enumerate(chosen):
            left = shot_hit if slot is None else [a * b for a, b in zip(shot_hit, row(source, slot))]
            got = nt(jnp.concatenate(left, axis=1), point_hit)
            into_ref[c] = jnp.where(s == 0, got, into_ref[c] + got)

    for half in range(halves):

        def step(s, carry):
            source = s * halves + half
            shot_hit = hits(source, shots, cols + 2, 0.0)
            point_hit = jnp.concatenate(hits(source, points, cols + 3, 0.0), axis=1)
            summed(acc_ref, s, source, shot_hit, point_hit, list(range(cols)) + [None])
            return carry

        lax.fori_loop(0, sources, step, 0)
        scale = 1.0 / jnp.maximum(acc_ref[cols], 1.0)
        for c in range(cols):
            panel_ref[c, :, half * points : (half + 1) * points] = (acc_ref[c] * scale).astype(jnp.bfloat16)

    def top_step(s, carry):
        source = s * halves + own_half
        shot_hit = hits(source, shots, cols + 2, 0.0)
        point_hit = jnp.concatenate(hits(source, width, cols + 3, (own_shot * width).astype(jnp.float32)), axis=1)
        summed(top_acc_ref, s, source, shot_hit, point_hit, [cols, cols + 1, None])
        return carry

    lax.fori_loop(0, sources, top_step, 0)
    scale = 1.0 / jnp.maximum(top_acc_ref[2], 1.0)
    real = (top_acc_ref[0] * scale).astype(jnp.bfloat16)
    imag = (top_acc_ref[1] * scale).astype(jnp.bfloat16)
    dot = functools.partial(jnp.dot, preferred_element_type=jnp.float32)
    own_real, own_imag = own_ref[0], own_ref[1]
    out_real = dot(real, own_real) - dot(imag, own_imag)
    out_imag = dot(real, own_imag) + dot(imag, own_real)
    targets = top_ref.shape[0]
    block = shots // targets
    for t in range(targets):
        rows = slice(t * block, (t + 1) * block)
        top_ref[t] = jnp.concatenate([out_real[rows], out_imag[rows]], axis=0).astype(jnp.bfloat16)


def product_kernel(n_shot, across, halves, width, panel_ref, recv_ref, top_ref, out_ref):
    per, shots = panel_ref.shape[0] // 2, panel_ref.shape[1]
    lanes = recv_ref.shape[2]
    block = shots // (n_shot * halves)
    for f in range(per):
        left = panel_ref[2 * f : 2 * f + 2].reshape(2 * shots, panel_ref.shape[2])
        sides = []
        for c in range(2):
            first = (2 * f + c) * width
            blocks = [
                jnp.concatenate(
                    [
                        recv_ref[(s * across + r) * halves + h, first : first + width, :]
                        for h in range(halves)
                        for s in range(n_shot)
                    ],
                    axis=0,
                )
                for r in range(across)
            ]
            right = blocks[0] if across == 1 else jnp.concatenate(blocks, axis=1)
            sides.append(jnp.dot(left, right, preferred_element_type=jnp.float32))
        real = sides[0][:shots] - sides[1][shots:]
        imag = sides[1][:shots] + sides[0][shots:]
        for s in range(n_shot):
            for h in range(halves):
                first = (s * halves + h) * block
                both = jnp.concatenate([real[first : first + block], imag[first : first + block]], axis=0)
                for r in range(across):
                    part = both[:, r * lanes : (r + 1) * lanes].astype(jnp.bfloat16)
                    out_ref[(s * across + r) * halves + h, 2 * f * block : 2 * (f + 1) * block, :] = part
    mine = lax.axis_index("rcv") if across > 1 else 0
    for s in range(n_shot):
        for h in range(halves):
            for r in range(across):
                part = top_ref[s * halves + h]
                part = jnp.where(mine == r, part, jnp.zeros_like(part))
                out_ref[(s * across + r) * halves + h, 2 * per * block :, :] = part


def gather_kernel(per, got_ref, out_ref):
    block = out_ref.shape[2]
    sources = got_ref.shape[0]
    total = got_ref[0, 2 * per * block :, :].astype(jnp.float32)
    for g in range(1, sources):
        total = total + got_ref[g, 2 * per * block :, :].astype(jnp.float32)
    for g in range(sources):
        out_ref[g * per : (g + 1) * per] = got_ref[g, : 2 * per * block, :].reshape((per,) + out_ref.shape[1:])
    out_ref[sources * per :] = total.astype(jnp.bfloat16).reshape((1,) + out_ref.shape[1:])


def call(kernel, out_shape, operands, scratch=(), limit=LIMIT):
    return pl.pallas_call(
        kernel,
        out_shape=out_shape,
        in_specs=[VMEM] * len(operands),
        out_specs=jax.tree.map(lambda _: VMEM, out_shape),
        scratch_shapes=list(scratch),
        compiler_params=pltpu.CompilerParams(vmem_limit_bytes=limit),
    )(*operands)


def local(traces, trace_block, trace_shot, trace_point, recv_panel):
    n_shot, n_rcv, halves = lax.axis_size("shot"), lax.axis_size("rcv"), lax.axis_size("surf")
    freqs, _, width, lanes = recv_panel.shape
    window, n_rows = traces.shape[2], traces.shape[1]
    shots, points = SHOTS_PER_INDEX * n_shot, width * n_shot
    assert max(shots, points) <= 256
    main = freqs - 1
    pairs = n_shot * halves
    across = n_rcv if main % (pairs * n_rcv) == 0 else 1
    axes = ("shot", "rcv", "surf") if across > 1 else ("shot", "surf")
    groups = pairs * across
    per = main // groups
    cols = 2 * per
    block = shots // pairs
    bf16 = functools.partial(jax.ShapeDtypeStruct, dtype=jnp.bfloat16)
    high, low, slots = dft_tables(window, n_shot, across, halves, per, main)

    recv = recv_panel[:main].reshape(groups, per * 2 * width, lanes)
    recv = lax.all_to_all(recv, axes, split_axis=0, concat_axis=0, tiled=True)

    message = call(
        functools.partial(spectra_kernel, slots),
        bf16((pairs, n_rows // LANES * slots, LANES)),
        (traces[0], high, low, trace_block.reshape(1, n_rows), trace_shot, trace_point),
        limit=56 * 1024 * 1024,
    )
    rows = lax.all_to_all(message, ("shot", "surf"), split_axis=0, concat_axis=0, tiled=True)

    panel, top = call(
        functools.partial(bin_kernel, halves, shots, points, cols),
        (bf16((cols, shots, halves * points)), bf16((pairs, 2 * block, lanes))),
        (rows, recv_panel[main]),
        (pltpu.VMEM((cols + 1, shots, points), jnp.float32), pltpu.VMEM((3, shots, width), jnp.float32)),
    )
    out = call(
        functools.partial(product_kernel, n_shot, across, halves, width),
        bf16((groups, (per + 1) * 2 * block, lanes)),
        (panel, recv, top),
    )
    out = lax.all_to_all(out, axes, split_axis=0, concat_axis=0, tiled=True)
    return call(functools.partial(gather_kernel, per), bf16((freqs, 2, block, lanes)), (out,))


def solution(mesh):
    in_specs = (
        P("surf", "shot", None),
        P("surf", "shot", None),
        P("surf", "shot"),
        P("surf", "shot"),
        P(None, None, ("shot", "surf"), "rcv"),
    )
    out_specs = P(None, None, ("shot", "surf"), "rcv")
    return jax.shard_map(local, mesh=mesh, in_specs=in_specs, out_specs=out_specs, check_vma=False)
```

```python
import functools
import math

import jax
import jax.numpy as jnp
import numpy as np
from jax import lax
from jax.experimental import pallas as pl
from jax.experimental.pallas import tpu as pltpu
from jax.sharding import Mesh
from jax.sharding import PartitionSpec as P

SHOTS_PER_INDEX = 16
VMEM = pl.BlockSpec(memory_space=pltpu.VMEM)
LANES = 128
LIMIT = 16 * 1024 * 1024


GROUPS = 2
STACK = 5
SHOT = ("group", "member")


def dft_tables(window, members, n_rcv, per, top):
    slots = -(-(2 * per + 4) // 16) * 16
    n = np.arange(window, dtype=np.int64)
    table = np.zeros((n_rcv, members, slots, window), np.float64)
    for r in range(n_rcv):
        for t in range(members):
            first = (t * n_rcv + r) * per
            for j, f in enumerate(list(range(first, first + per)) + [top]):
                angle = (n * f % window) * (2.0 * math.pi / window)
                table[r, t, 2 * j] = np.cos(angle)
                table[r, t, 2 * j + 1] = -np.sin(angle)
    table = (table / math.sqrt(window)).astype(np.float32)
    high = table.astype(jnp.bfloat16)
    low = (table - high.astype(np.float32)).astype(jnp.bfloat16)
    return jnp.asarray(high), jnp.asarray(low)


def nt(a, b):
    return lax.dot_general(a, b, (((1,), (1,)), ((), ())), preferred_element_type=jnp.float32)


def spectra_kernel(cols, x_ref, high_ref, low_ref, block_ref, shot_ref, point_ref, *out_refs):
    x = x_ref[...]
    mine, member = lax.axis_index("rcv"), lax.axis_index("member")
    high = jnp.concatenate([high_ref[mine, member ^ d] for d in range(len(out_refs))], axis=0)
    low = jnp.concatenate([low_ref[mine, member ^ d] for d in range(len(out_refs))], axis=0)
    y = nt(high, x) + nt(low, x)
    slots = high_ref.shape[2]
    shot = (block_ref[...] * SHOTS_PER_INDEX + shot_ref[...]).astype(jnp.float32)
    point = point_ref[...].astype(jnp.float32)
    for d, out_ref in enumerate(out_refs):
        pieces = []
        for j in range(x.shape[0] // LANES):
            lanes = slice(j * LANES, (j + 1) * LANES)
            pieces += [y[d * slots : d * slots + cols + 2, lanes], shot[:, lanes], point[:, lanes]]
        out_ref[...] = jnp.concatenate(pieces, axis=0).astype(jnp.bfloat16)


def bin_kernel(halves, shots, points, cols, n_sources, *refs):
    row_refs, own_ref = refs[:n_sources], refs[n_sources]
    panel_refs = refs[n_sources + 1 : n_sources + 1 + halves]
    top_ref, rows_ref, left_ref, acc_ref, pad_ref = refs[n_sources + 1 + halves :]
    width = own_ref.shape[1]
    slots = cols + 4
    parts = row_refs[0].shape[0] // slots
    group, member, own_half = (lax.axis_index(name) for name in ("group", "member", "surf"))
    for i, ref in enumerate(row_refs):
        rows_ref[i] = ref[...]
    acc_ref[...] = jnp.zeros_like(acc_ref)
    pad_ref[...] = jnp.zeros_like(pad_ref)
    pad_ref[:, pl.ds(pl.multiple_of(member * width, width), width), :] = own_ref[...]

    def hits(source, count, slot, first):
        grid = lax.broadcasted_iota(jnp.int32, (count, LANES), 0).astype(jnp.float32)
        ids = [rows_ref[source, j * slots + slot : j * slots + slot + 1, :] for j in range(parts)]
        return [jnp.where(grid == i.astype(jnp.float32) - first, 1.0, 0.0).astype(jnp.bfloat16) for i in ids]

    chosen = list(range(cols + 2)) + [None]

    def step(source, carry):
        shot_hit = hits(source, shots, cols + 2, 0.0)
        point_hit = jnp.concatenate(hits(source, points, cols + 3, (group * points).astype(jnp.float32)), axis=1)
        for first in range(0, len(chosen), STACK):
            stack = chosen[first : first + STACK]
            for i, slot in enumerate(stack):
                for j in range(parts):
                    left = shot_hit[j]
                    if slot is not None:
                        left = left * rows_ref[source, j * slots + slot : j * slots + slot + 1, :]
                    left_ref[i * shots : (i + 1) * shots, j * LANES : (j + 1) * LANES] = left
            got = nt(left_ref[: len(stack) * shots], point_hit)
            acc_ref[first : first + len(stack)] += got.reshape(len(stack), shots, points)
        return carry

    lax.fori_loop(0, n_sources, step, 0)
    scale = 1.0 / jnp.maximum(acc_ref[cols + 2], 1.0)
    each = cols // halves
    for k, ref in enumerate(panel_refs):
        for c in range(each):
            ref[c] = (acc_ref[(own_half ^ k) * each + c] * scale).astype(jnp.bfloat16)
    real = (acc_ref[cols] * scale).astype(jnp.bfloat16)
    imag = (acc_ref[cols + 1] * scale).astype(jnp.bfloat16)
    dot = functools.partial(jnp.dot, preferred_element_type=jnp.float32)
    out_real = dot(real, pad_ref[0]) - dot(imag, pad_ref[1])
    out_imag = dot(real, pad_ref[1]) + dot(imag, pad_ref[0])
    targets = top_ref.shape[0]
    block = shots // targets
    for t in range(targets):
        rows = slice(t * block, (t + 1) * block)
        top_ref[t] = jnp.concatenate([out_real[rows], out_imag[rows]], axis=0).astype(jnp.bfloat16)


def product_kernel(members, n_shot, n_rcv, halves, width, *refs):
    panel_refs, (recv_ref, top_ref, out_ref) = refs[:halves], refs[halves:]
    per, shots, points = panel_refs[0].shape[0] // 2, panel_refs[0].shape[1], panel_refs[0].shape[2]
    lanes = recv_ref.shape[2]
    block = shots // (n_shot * halves)
    own_half, mine = lax.axis_index("surf"), lax.axis_index("rcv")
    for f in range(per):
        left = [ref[2 * f : 2 * f + 2].reshape(2 * shots, points) for ref in panel_refs]
        left = jnp.concatenate(left, axis=1)
        sides = []
        for c in range(2):
            first = (2 * f + c) * width
            blocks = [
                jnp.concatenate(
                    [
                        recv_ref[(t * n_rcv + r) * halves + (own_half ^ k), first : first + width, :]
                        for k in range(halves)
                        for t in range(members)
                    ],
                    axis=0,
                )
                for r in range(n_rcv)
            ]
            right = blocks[0] if n_rcv == 1 else jnp.concatenate(blocks, axis=1)
            sides.append(jnp.dot(left, right, preferred_element_type=jnp.float32))
        real = sides[0][:shots] - sides[1][shots:]
        imag = sides[1][:shots] + sides[0][shots:]
        for s in range(n_shot):
            for h in range(halves):
                first = (s * halves + h) * block
                both = jnp.concatenate([real[first : first + block], imag[first : first + block]], axis=0)
                for r in range(n_rcv):
                    part = both[:, r * lanes : (r + 1) * lanes].astype(jnp.bfloat16)
                    out_ref[(s * n_rcv + r) * halves + h, 2 * f * block : 2 * (f + 1) * block, :] = part
    for s in range(n_shot):
        for h in range(halves):
            for r in range(n_rcv):
                part = top_ref[s * halves + h]
                part = jnp.where(mine == r, part, jnp.zeros_like(part))
                out_ref[(s * n_rcv + r) * halves + h, 2 * per * block :, :] = part


def gather_kernel(per, groups, got_ref, out_ref):
    block = out_ref.shape[2]
    each = got_ref.shape[0] // groups
    rows = 2 * per * block
    total = jnp.zeros((2 * block, got_ref.shape[2]), jnp.float32)
    for w in range(each):
        value = jnp.zeros((rows, got_ref.shape[2]), jnp.float32)
        for g in range(groups):
            value = value + got_ref[g * each + w, :rows, :].astype(jnp.float32)
            total = total + got_ref[g * each + w, rows:, :].astype(jnp.float32)
        out_ref[w * per : (w + 1) * per] = value.reshape((per,) + out_ref.shape[1:]).astype(jnp.bfloat16)
    out_ref[each * per :] = total.reshape((1,) + out_ref.shape[1:]).astype(jnp.bfloat16)


def call(kernel, out_shape, operands, scratch=(), limit=LIMIT):
    return pl.pallas_call(
        kernel,
        out_shape=out_shape,
        in_specs=[VMEM] * len(operands),
        out_specs=jax.tree.map(lambda _: VMEM, out_shape),
        scratch_shapes=list(scratch),
        compiler_params=pltpu.CompilerParams(vmem_limit_bytes=limit),
    )(*operands)


def local(traces, trace_block, trace_shot, trace_point, recv_panel):
    groups, members = lax.axis_size("group"), lax.axis_size("member")
    n_shot, n_rcv, halves = groups * members, lax.axis_size("rcv"), lax.axis_size("surf")
    freqs, _, width, lanes = recv_panel.shape
    window, n_rows = traces.shape[2], traces.shape[1]
    shots, points = SHOTS_PER_INDEX * n_shot, width * members
    assert max(shots, points * groups) <= 256
    main = freqs - 1
    owners = members * n_rcv * halves
    per = main // owners
    assert per * owners == main
    cols = 2 * per * halves
    block = shots // (n_shot * halves)
    bf16 = functools.partial(jax.ShapeDtypeStruct, dtype=jnp.bfloat16)
    high, low = dft_tables(window, members, n_rcv, per * halves, main)

    messages = call(
        functools.partial(spectra_kernel, cols),
        (bf16((n_rows // LANES * (cols + 4), LANES)),) * members,
        (traces[0], high, low, trace_block.reshape(1, n_rows), trace_shot, trace_point),
        limit=56 * 1024 * 1024,
    )
    rows = [messages[0]]
    for d in range(1, n_shot):
        rows.append(lax.ppermute(messages[d % members], SHOT, [(s, s ^ d) for s in range(n_shot)]))

    recv = recv_panel[:main].reshape(owners, per * 2 * width, lanes)
    recv, *rows = lax.optimization_barrier((recv, *rows))
    recv = lax.all_to_all(recv, ("member", "rcv", "surf"), split_axis=0, concat_axis=0, tiled=True)

    panel = bf16((2 * per, shots, points))
    *panels, top = call(
        functools.partial(bin_kernel, halves, shots, points, cols, n_shot),
        (panel,) * halves + (bf16((n_shot * halves, 2 * block, lanes)),),
        (*rows, recv_panel[main]),
        (
            pltpu.VMEM((n_shot,) + rows[0].shape, jnp.bfloat16),
            pltpu.VMEM((STACK * shots, n_rows), jnp.bfloat16),
            pltpu.VMEM((cols + 3, shots, points), jnp.float32),
            pltpu.VMEM((2, points, lanes), jnp.bfloat16),
        ),
    )
    for k in range(1, halves):
        panels[k] = lax.ppermute(panels[k], "surf", [(h, h ^ k) for h in range(halves)])
    out = call(
        functools.partial(product_kernel, members, n_shot, n_rcv, halves, width),
        bf16((n_shot * n_rcv * halves, (per + 1) * 2 * block, lanes)),
        (*panels, recv, top),
    )
    out = lax.all_to_all(out, SHOT + ("rcv", "surf"), split_axis=0, concat_axis=0, tiled=True)
    return call(functools.partial(gather_kernel, per, groups), bf16((freqs, 2, block, lanes)), (out,))


def solution(mesh):
    n_shot, n_rcv, halves = (mesh.shape[name] for name in ("shot", "rcv", "surf"))
    devices = mesh.devices.reshape(GROUPS, n_shot // GROUPS, n_rcv, halves)
    mesh = Mesh(devices, SHOT + ("rcv", "surf"))
    in_specs = (
        P("surf", SHOT, None),
        P("surf", SHOT, None),
        P("surf", SHOT),
        P("surf", SHOT),
        P(None, None, SHOT + ("surf",), "rcv"),
    )
    out_specs = P(None, None, SHOT + ("surf",), "rcv")
    return jax.shard_map(local, mesh=mesh, in_specs=in_specs, out_specs=out_specs, check_vma=False)
```

```python
import functools
import math

import jax
import jax.numpy as jnp
import numpy as np
from jax import lax
from jax.experimental import pallas as pl
from jax.experimental.pallas import tpu as pltpu
from jax.sharding import Mesh
from jax.sharding import PartitionSpec as P

SHOTS_PER_INDEX = 16
VMEM = pl.BlockSpec(memory_space=pltpu.VMEM)
LANES = 128
LIMIT = 16 * 1024 * 1024


GROUPS = 2
NEAR, FAR = 12, 12
STACK = 5
SHOT = ("group", "member")


def dft_tables(window, members, n_rcv, per, top):
    slots = -(-(2 * per + 4) // 16) * 16
    n = np.arange(window, dtype=np.int64)
    table = np.zeros((n_rcv, members, slots, window), np.float64)
    for r in range(n_rcv):
        for t in range(members):
            first = (t * n_rcv + r) * per
            for j, f in enumerate(list(range(first, first + per)) + [top]):
                angle = (n * f % window) * (2.0 * math.pi / window)
                table[r, t, 2 * j] = np.cos(angle)
                table[r, t, 2 * j + 1] = -np.sin(angle)
    table = (table / math.sqrt(window)).astype(np.float32)
    high = table.astype(jnp.bfloat16)
    low = (table - high.astype(np.float32)).astype(jnp.bfloat16)
    return jnp.asarray(high), jnp.asarray(low)


def nt(a, b):
    return lax.dot_general(a, b, (((1,), (1,)), ((), ())), preferred_element_type=jnp.float32)


def spectra_kernel(cols, x_ref, high_ref, low_ref, block_ref, shot_ref, point_ref, *out_refs):
    x = x_ref[...]
    mine, member = lax.axis_index("rcv"), lax.axis_index("member")
    slots = high_ref.shape[2]
    y = nt(jnp.concatenate([ref[mine, member ^ d] for ref in (high_ref, low_ref) for d in range(len(out_refs))], axis=0), x)
    y = y[: slots * len(out_refs)] + y[slots * len(out_refs) :]
    shot = (block_ref[...] * SHOTS_PER_INDEX + shot_ref[...]).astype(jnp.float32)
    point = point_ref[...].astype(jnp.float32)
    for d, out_ref in enumerate(out_refs):
        pieces = []
        for j in range(x.shape[0] // LANES):
            lanes = slice(j * LANES, (j + 1) * LANES)
            pieces += [y[d * slots : d * slots + cols + 2, lanes], shot[:, lanes], point[:, lanes]]
        out_ref[...] = jnp.concatenate(pieces, axis=0).astype(jnp.bfloat16)


def add_rows(cols, rows_ref, left_ref, acc_ref):
    _, shots, points = acc_ref.shape
    slots = cols + 4
    parts = rows_ref.shape[1] // slots
    group = lax.axis_index("group")

    def hits(source, count, slot, first):
        grid = lax.broadcasted_iota(jnp.int32, (count, LANES), 0).astype(jnp.float32)
        ids = [rows_ref[source, j * slots + slot : j * slots + slot + 1, :] for j in range(parts)]
        return [jnp.where(grid == i.astype(jnp.float32) - first, 1.0, 0.0).astype(jnp.bfloat16) for i in ids]

    chosen = list(range(cols + 2)) + [None]

    def step(source, carry):
        shot_hit = hits(source, shots, cols + 2, 0.0)
        point_hit = jnp.concatenate(hits(source, points, cols + 3, (group * points).astype(jnp.float32)), axis=1)
        for first in range(0, len(chosen), STACK):
            stack = chosen[first : first + STACK]
            for i, slot in enumerate(stack):
                for j in range(parts):
                    left = shot_hit[j]
                    if slot is not None:
                        left = left * rows_ref[source, j * slots + slot : j * slots + slot + 1, :]
                    left_ref[i * shots : (i + 1) * shots, j * LANES : (j + 1) * LANES] = left
            got = nt(left_ref[: len(stack) * shots], point_hit)
            acc_ref[first : first + len(stack)] += got.reshape(len(stack), shots, points)
        return carry

    lax.fori_loop(0, rows_ref.shape[0], step, 0)


def near_kernel(cols, rows_ref, acc_ref, left_ref):
    acc_ref[...] = jnp.zeros_like(acc_ref)
    add_rows(cols, rows_ref, left_ref, acc_ref)


def far_kernel(cols, halves, rows_ref, near_ref, own_ref, *refs):
    panel_refs, (left_ref, acc_ref, pad_ref) = refs[:halves], refs[halves:]
    width = own_ref.shape[1]
    member, own_half = lax.axis_index("member"), lax.axis_index("surf")
    pad_ref[...] = jnp.zeros_like(pad_ref)
    pad_ref[:, pl.ds(pl.multiple_of(member * width, width), width), :] = own_ref[...]
    acc_ref[...] = near_ref[...]
    add_rows(cols, rows_ref, left_ref, acc_ref)
    scale = 1.0 / jnp.maximum(acc_ref[cols + 2], 1.0)
    each = cols // halves
    for k, ref in enumerate(panel_refs):
        for c in range(each):
            ref[c] = (acc_ref[(own_half ^ k) * each + c] * scale).astype(jnp.bfloat16)
    real = (acc_ref[cols] * scale).astype(jnp.bfloat16)
    imag = (acc_ref[cols + 1] * scale).astype(jnp.bfloat16)
    dot = functools.partial(jnp.dot, preferred_element_type=jnp.float32)
    out_real = dot(real, pad_ref[0]) - dot(imag, pad_ref[1])
    out_imag = dot(real, pad_ref[1]) + dot(imag, pad_ref[0])
    for ref in panel_refs:
        ref[each] = out_real.astype(jnp.bfloat16)
        ref[each + 1] = out_imag.astype(jnp.bfloat16)


def product_kernel(members, n_shot, n_rcv, halves, width, *refs):
    panel_refs, (recv_ref, out_ref) = refs[:halves], refs[halves:]
    per, shots, points = panel_refs[0].shape[0] // 2 - 1, panel_refs[0].shape[1], panel_refs[0].shape[2]
    lanes = recv_ref.shape[2]
    block = shots // (n_shot * halves)
    own_half, mine = lax.axis_index("surf"), lax.axis_index("rcv")
    for f in range(per):
        left = [ref[2 * f : 2 * f + 2].reshape(2 * shots, points) for ref in panel_refs]
        left = jnp.concatenate(left, axis=1)
        sides = []
        for c in range(2):
            first = (2 * f + c) * width
            blocks = [
                jnp.concatenate(
                    [
                        recv_ref[(t * n_rcv + r) * halves + (own_half ^ k), first : first + width, :]
                        for k in range(halves)
                        for t in range(members)
                    ],
                    axis=0,
                )
                for r in range(n_rcv)
            ]
            right = blocks[0] if n_rcv == 1 else jnp.concatenate(blocks, axis=1)
            sides.append(jnp.dot(left, right, preferred_element_type=jnp.float32))
        real = sides[0][:shots] - sides[1][shots:]
        imag = sides[1][:shots] + sides[0][shots:]
        for s in range(n_shot):
            for h in range(halves):
                first = (s * halves + h) * block
                both = jnp.concatenate([real[first : first + block], imag[first : first + block]], axis=0)
                for r in range(n_rcv):
                    part = both[:, r * lanes : (r + 1) * lanes].astype(jnp.bfloat16)
                    out_ref[(s * n_rcv + r) * halves + h, 2 * f * block : 2 * (f + 1) * block, :] = part
    top = panel_refs[0][2 * per + own_half].astype(jnp.float32)
    for ref in panel_refs[1:]:
        top = top + ref[2 * per + own_half].astype(jnp.float32)
    for r in range(n_rcv):
        part = jnp.where(mine == r, top, jnp.zeros_like(top)).astype(jnp.bfloat16)
        for s in range(n_shot):
            for h in range(halves):
                first = (s * halves + h) * block
                out_ref[(s * n_rcv + r) * halves + h, 2 * per * block :, :] = part[first : first + block]


def gather_kernel(per, groups, halves, got_ref, out_ref):
    block = out_ref.shape[2]
    each = got_ref.shape[0] // groups
    rows = 2 * per * block
    tops = [jnp.zeros((block, got_ref.shape[2]), jnp.float32) for _ in range(halves)]
    for w in range(each):
        value = jnp.zeros((rows, got_ref.shape[2]), jnp.float32)
        for g in range(groups):
            value = value + got_ref[g * each + w, :rows, :].astype(jnp.float32)
            tops[w % halves] = tops[w % halves] + got_ref[g * each + w, rows:, :].astype(jnp.float32)
        out_ref[w * per : (w + 1) * per] = value.reshape((per,) + out_ref.shape[1:]).astype(jnp.bfloat16)
    for c in range(halves):
        out_ref[each * per, c] = tops[c].astype(jnp.bfloat16)


def call(kernel, out_shape, operands, scratch=(), limit=LIMIT, flops=None):
    return pl.pallas_call(
        kernel,
        out_shape=out_shape,
        in_specs=[VMEM] * len(operands),
        out_specs=jax.tree.map(lambda _: VMEM, out_shape),
        scratch_shapes=list(scratch),
        compiler_params=pltpu.CompilerParams(vmem_limit_bytes=limit),
        cost_estimate=flops and pl.CostEstimate(flops=flops, transcendentals=0, bytes_accessed=0),
    )(*operands)


def local(traces, trace_block, trace_shot, trace_point, recv_panel):
    groups, members = lax.axis_size("group"), lax.axis_size("member")
    n_shot, n_rcv, halves = groups * members, lax.axis_size("rcv"), lax.axis_size("surf")
    freqs, _, width, lanes = recv_panel.shape
    window, n_rows = traces.shape[2], traces.shape[1]
    shots, points = SHOTS_PER_INDEX * n_shot, width * members
    assert max(shots, points * groups) <= 256
    main = freqs - 1
    owners = members * n_rcv * halves
    per = main // owners
    assert per * owners == main and halves == 2 and points == lanes
    cols = 2 * per * halves
    block = shots // (n_shot * halves)
    bf16 = functools.partial(jax.ShapeDtypeStruct, dtype=jnp.bfloat16)
    high, low = dft_tables(window, members, n_rcv, per * halves, main)

    message = bf16((n_rows // LANES * (cols + 4), LANES))
    messages = call(
        functools.partial(spectra_kernel, cols),
        (message,) * members,
        (traces[0], high, low, trace_block.reshape(1, n_rows), trace_shot, trace_point),
        limit=56 * 1024 * 1024,
    )
    near = [messages[0]]
    for d in range(members - 1, 0, -1):
        near.append(lax.ppermute(messages[d], "member", [(t, t ^ d) for t in range(members)]))
    near = jnp.stack(near)
    far = lax.ppermute(near, "group", [(g, g ^ 1) for g in range(groups)])

    recv = recv_panel[:main].reshape(owners, per * 2 * width, lanes)
    recv, near = lax.optimization_barrier((recv, near))
    recv = lax.all_to_all(recv, ("member", "rcv", "surf"), split_axis=0, concat_axis=0, tiled=True)

    acc = jax.ShapeDtypeStruct((cols + 3, shots, points), jnp.float32)
    left = pltpu.VMEM((STACK * shots, n_rows), jnp.bfloat16)
    work = (cols + 3) * shots * points * n_rows * members
    acc_near = call(functools.partial(near_kernel, cols), acc, (near,), (left,), flops=NEAR * work)
    panels = call(
        functools.partial(far_kernel, cols, halves),
        (bf16((2 * per + 2, shots, points)),) * halves,
        (far, acc_near, recv_panel[main]),
        (left, pltpu.VMEM(acc.shape, jnp.float32), pltpu.VMEM((2, points, lanes), jnp.bfloat16)),
        flops=FAR * work,
    )
    panels = list(panels)
    for k in range(1, halves):
        panels[k] = lax.ppermute(panels[k], "surf", [(h, h ^ k) for h in range(halves)])
    out = call(
        functools.partial(product_kernel, members, n_shot, n_rcv, halves, width),
        bf16((n_shot * n_rcv * halves, (2 * per + 1) * block, lanes)),
        (*panels, recv),
    )
    out = lax.all_to_all(out, SHOT + ("rcv", "surf"), split_axis=0, concat_axis=0, tiled=True)
    return call(functools.partial(gather_kernel, per, groups, halves), bf16((freqs, 2, block, lanes)), (out,))


def solution(mesh):
    n_shot, n_rcv, halves = (mesh.shape[name] for name in ("shot", "rcv", "surf"))
    devices = mesh.devices.reshape(GROUPS, n_shot // GROUPS, n_rcv, halves)
    mesh = Mesh(devices, SHOT + ("rcv", "surf"))
    in_specs = (
        P("surf", SHOT, None),
        P("surf", SHOT, None),
        P("surf", SHOT),
        P("surf", SHOT),
        P(None, None, SHOT + ("surf",), "rcv"),
    )
    out_specs = P(None, None, SHOT + ("surf",), "rcv")
    return jax.shard_map(local, mesh=mesh, in_specs=in_specs, out_specs=out_specs, check_vma=False)
```

```python
import functools
import math

import jax
import jax.numpy as jnp
import numpy as np
from jax import lax
from jax.experimental import pallas as pl
from jax.experimental.pallas import tpu as pltpu
from jax.sharding import Mesh
from jax.sharding import PartitionSpec as P

SHOTS_PER_INDEX = 16
VMEM = pl.BlockSpec(memory_space=pltpu.VMEM)
LANES = 128
LIMIT = 16 * 1024 * 1024


GROUPS = 2
HEAD = 1
HEAD_COST, NEAR_COST, FAR_COST = 48, 24, 24
STACK = 7
SHOT = ("group", "member")


def share_of(group, member, members):
    return member ^ (group * (members // 2))


def dft_tables(window, members, n_rcv, per, top):
    slots = -(-(2 * per + 4) // 16) * 16
    n = np.arange(window, dtype=np.int64)
    table = np.zeros((n_rcv, members, slots, window), np.float64)
    for r in range(n_rcv):
        for t in range(members):
            first = (t * n_rcv + r) * per
            for j, f in enumerate(list(range(first, first + per)) + [top]):
                angle = (n * f % window) * (2.0 * math.pi / window)
                table[r, t, 2 * j] = np.cos(angle)
                table[r, t, 2 * j + 1] = -np.sin(angle)
    table = (table / math.sqrt(window)).astype(np.float32)
    high = table.astype(jnp.bfloat16)
    low = (table - high.astype(np.float32)).astype(jnp.bfloat16)
    return jnp.asarray(high), jnp.asarray(low)


def nt(a, b):
    return lax.dot_general(a, b, (((1,), (1,)), ((), ())), preferred_element_type=jnp.float32)


def spectra_kernel(cols, x_ref, high_ref, low_ref, block_ref, shot_ref, point_ref, *out_refs):
    x = x_ref[...]
    mine, first = lax.axis_index("rcv"), share_of(lax.axis_index("group"), lax.axis_index("member"), high_ref.shape[1])
    slots = high_ref.shape[2]
    y = nt(jnp.concatenate([ref[mine, first ^ d] for ref in (high_ref, low_ref) for d in range(len(out_refs))], axis=0), x)
    y = y[: slots * len(out_refs)] + y[slots * len(out_refs) :]
    shot = (block_ref[...] * SHOTS_PER_INDEX + shot_ref[...]).astype(jnp.float32)
    point = point_ref[...].astype(jnp.float32)
    for d, out_ref in enumerate(out_refs):
        pieces = []
        for j in range(x.shape[0] // LANES):
            lanes = slice(j * LANES, (j + 1) * LANES)
            pieces += [y[d * slots : d * slots + cols + 2, lanes], shot[:, lanes], point[:, lanes]]
        out_ref[...] = jnp.concatenate(pieces, axis=0).astype(jnp.bfloat16)


def add_rows(cols, rows_ref, first_source, last_source, left_ref, acc_ref):
    _, shots, points = acc_ref.shape
    slots = cols + 4
    parts = rows_ref.shape[1] // slots
    group = lax.axis_index("group")

    def hits(source, count, slot, first):
        grid = lax.broadcasted_iota(jnp.int32, (count, LANES), 0).astype(jnp.float32)
        ids = [rows_ref[source, j * slots + slot : j * slots + slot + 1, :] for j in range(parts)]
        return [jnp.where(grid == i.astype(jnp.float32) - first, 1.0, 0.0).astype(jnp.bfloat16) for i in ids]

    chosen = list(range(cols + 2)) + [None]

    def step(source, carry):
        shot_hit = hits(source, shots, cols + 2, 0.0)
        point_hit = jnp.concatenate(hits(source, points, cols + 3, (group * points).astype(jnp.float32)), axis=1)
        for first in range(0, len(chosen), STACK):
            stack = chosen[first : first + STACK]
            for i, slot in enumerate(stack):
                for j in range(parts):
                    left = shot_hit[j]
                    if slot is not None:
                        left = left * rows_ref[source, j * slots + slot : j * slots + slot + 1, :]
                    left_ref[i * shots : (i + 1) * shots, j * LANES : (j + 1) * LANES] = left
            got = nt(left_ref[: len(stack) * shots], point_hit)
            acc_ref[first : first + len(stack)] += got.reshape(len(stack), shots, points)
        return carry

    lax.fori_loop(first_source, last_source, step, 0)


def near_kernel(cols, first, last, rows_ref, *refs):
    *before, acc_ref, left_ref = refs
    acc_ref[...] = before[0][...] if before else jnp.zeros_like(acc_ref)
    add_rows(cols, rows_ref, first, last, left_ref, acc_ref)


def far_kernel(cols, halves, outer_ref, inner_ref, near_ref, own_ref, *refs):
    panel_refs, (rows_ref, left_ref, acc_ref, pad_ref) = refs[:halves], refs[halves:]
    width = own_ref.shape[1]
    member, own_half = lax.axis_index("member"), lax.axis_index("surf")
    pad_ref[...] = jnp.zeros_like(pad_ref)
    pad_ref[:, pl.ds(pl.multiple_of(member * width, width), width), :] = own_ref[...]
    acc_ref[...] = near_ref[...]
    rows_ref[...] = outer_ref[...] + inner_ref[...]
    add_rows(cols, rows_ref, 0, rows_ref.shape[0], left_ref, acc_ref)
    scale = 1.0 / jnp.maximum(acc_ref[cols + 2], 1.0)
    each = cols // halves
    for k, ref in enumerate(panel_refs):
        for c in range(each):
            ref[c] = (acc_ref[(own_half ^ k) * each + c] * scale).astype(jnp.bfloat16)
    real = (acc_ref[cols] * scale).astype(jnp.bfloat16)
    imag = (acc_ref[cols + 1] * scale).astype(jnp.bfloat16)
    dot = functools.partial(jnp.dot, preferred_element_type=jnp.float32)
    out_real = dot(real, pad_ref[0]) - dot(imag, pad_ref[1])
    out_imag = dot(real, pad_ref[1]) + dot(imag, pad_ref[0])
    for ref in panel_refs:
        ref[each] = out_real.astype(jnp.bfloat16)
        ref[each + 1] = out_imag.astype(jnp.bfloat16)


def product_kernel(members, n_shot, n_rcv, halves, width, *refs):
    panel_refs, (recv_ref, out_ref) = refs[:halves], refs[halves:]
    per, shots, points = panel_refs[0].shape[0] // 2 - 1, panel_refs[0].shape[1], panel_refs[0].shape[2]
    lanes = recv_ref.shape[2]
    block = shots // (n_shot * halves)
    own_half, mine = lax.axis_index("surf"), lax.axis_index("rcv")
    for f in range(per):
        left = [ref[2 * f : 2 * f + 2].reshape(2 * shots, points) for ref in panel_refs]
        left = jnp.concatenate(left, axis=1)
        sides = []
        for c in range(2):
            first = (2 * f + c) * width
            blocks = [
                jnp.concatenate(
                    [
                        recv_ref[(t * n_rcv + r) * halves + (own_half ^ k), first : first + width, :]
                        for k in range(halves)
                        for t in range(members)
                    ],
                    axis=0,
                )
                for r in range(n_rcv)
            ]
            right = blocks[0] if n_rcv == 1 else jnp.concatenate(blocks, axis=1)
            sides.append(jnp.dot(left, right, preferred_element_type=jnp.float32))
        real = sides[0][:shots] - sides[1][shots:]
        imag = sides[1][:shots] + sides[0][shots:]
        for s in range(n_shot):
            for h in range(halves):
                first = (s * halves + h) * block
                both = jnp.concatenate([real[first : first + block], imag[first : first + block]], axis=0)
                for r in range(n_rcv):
                    part = both[:, r * lanes : (r + 1) * lanes].astype(jnp.bfloat16)
                    out_ref[(s * n_rcv + r) * halves + h, 2 * f * block : 2 * (f + 1) * block, :] = part
    top = panel_refs[0][2 * per + own_half].astype(jnp.float32)
    for ref in panel_refs[1:]:
        top = top + ref[2 * per + own_half].astype(jnp.float32)
    for r in range(n_rcv):
        part = jnp.where(mine == r, top, jnp.zeros_like(top)).astype(jnp.bfloat16)
        for s in range(n_shot):
            for h in range(halves):
                first = (s * halves + h) * block
                out_ref[(s * n_rcv + r) * halves + h, 2 * per * block :, :] = part[first : first + block]


def gather_kernel(per, groups, halves, got_ref, out_ref):
    block = out_ref.shape[2]
    each = got_ref.shape[0] // groups
    rows = 2 * per * block
    tops = [jnp.zeros((block, got_ref.shape[2]), jnp.float32) for _ in range(halves)]
    for w in range(each):
        value = jnp.zeros((rows, got_ref.shape[2]), jnp.float32)
        for g in range(groups):
            source = g * each + share_of(g, w, each)
            value = value + got_ref[source, :rows, :].astype(jnp.float32)
            tops[w % halves] = tops[w % halves] + got_ref[source, rows:, :].astype(jnp.float32)
        out_ref[w * per : (w + 1) * per] = value.reshape((per,) + out_ref.shape[1:]).astype(jnp.bfloat16)
    for c in range(halves):
        out_ref[each * per, c] = tops[c].astype(jnp.bfloat16)


def call(kernel, out_shape, operands, scratch=(), limit=LIMIT, flops=None):
    return pl.pallas_call(
        kernel,
        out_shape=out_shape,
        in_specs=[VMEM] * len(operands),
        out_specs=jax.tree.map(lambda _: VMEM, out_shape),
        scratch_shapes=list(scratch),
        compiler_params=pltpu.CompilerParams(vmem_limit_bytes=limit),
        cost_estimate=flops and pl.CostEstimate(flops=flops, transcendentals=0, bytes_accessed=0),
    )(*operands)


def local(traces, trace_block, trace_shot, trace_point, recv_panel):
    groups, members = lax.axis_size("group"), lax.axis_size("member")
    n_shot, n_rcv, halves = groups * members, lax.axis_size("rcv"), lax.axis_size("surf")
    freqs, _, width, lanes = recv_panel.shape
    window, n_rows = traces.shape[2], traces.shape[1]
    shots, points = SHOTS_PER_INDEX * n_shot, width * members
    assert max(shots, points * groups) <= 256
    main = freqs - 1
    owners = members * n_rcv * halves
    per = main // owners
    assert per * owners == main and halves == 2 and points == lanes
    cols = 2 * per * halves
    block = shots // (n_shot * halves)
    bf16 = functools.partial(jax.ShapeDtypeStruct, dtype=jnp.bfloat16)
    high, low = dft_tables(window, members, n_rcv, per * halves, main)

    message = bf16((n_rows // LANES * (cols + 4), LANES))
    messages = call(
        functools.partial(spectra_kernel, cols),
        (message,) * members,
        (traces[0], high, low, trace_block.reshape(1, n_rows), trace_shot, trace_point),
        limit=56 * 1024 * 1024,
    )
    near = [messages[0]]
    for d in range(members - 1, 0, -1):
        near.append(lax.ppermute(messages[d], "member", [(t, t ^ d) for t in range(members)]))
    near = jnp.stack(near)
    pairs = [(m, members + share_of(1, m, members)) for m in range(members)]
    outer, inner = (chosen + [(b, a) for a, b in chosen] for chosen in (pairs[: members // 2], pairs[members // 2 :]))
    outer = lax.ppermute(near, SHOT, outer)

    share = main // 2
    swap = lax.axis_index("group") * share
    recv = [lax.dynamic_slice_in_dim(recv_panel, start, share, 0) for start in (swap, share - swap)]
    recv = jnp.concatenate(recv, axis=0).reshape(owners, per * 2 * width, lanes)
    recv, near = lax.optimization_barrier((recv, near))
    recv = lax.all_to_all(recv, ("member", "rcv", "surf"), split_axis=0, concat_axis=0, tiled=True)

    acc = jax.ShapeDtypeStruct((cols + 3, shots, points), jnp.float32)
    left = pltpu.VMEM((STACK * shots, n_rows), jnp.bfloat16)
    work = (cols + 3) * shots * points * n_rows
    acc_near = call(functools.partial(near_kernel, cols, 0, HEAD), acc, (near,), (left,), flops=HEAD_COST * work)
    tied, acc_near = lax.optimization_barrier((near, acc_near))
    inner = lax.ppermute(tied, SHOT, inner)
    acc_near = call(functools.partial(near_kernel, cols, HEAD, members), acc, (near, acc_near), (left,), flops=NEAR_COST * work)
    panels = call(
        functools.partial(far_kernel, cols, halves),
        (bf16((2 * per + 2, shots, points)),) * halves,
        (outer, inner, acc_near, recv_panel[main]),
        (pltpu.VMEM(near.shape, jnp.bfloat16), left, pltpu.VMEM(acc.shape, jnp.float32), pltpu.VMEM((2, points, lanes), jnp.bfloat16)),
        flops=FAR_COST * work,
    )
    panels = list(panels)
    for k in range(1, halves):
        panels[k] = lax.ppermute(panels[k], "surf", [(h, h ^ k) for h in range(halves)])
    out = call(
        functools.partial(product_kernel, members, n_shot, n_rcv, halves, width),
        bf16((n_shot * n_rcv * halves, (2 * per + 1) * block, lanes)),
        (*panels, recv),
    )
    out = lax.all_to_all(out, SHOT + ("rcv", "surf"), split_axis=0, concat_axis=0, tiled=True)
    return call(functools.partial(gather_kernel, per, groups, halves), bf16((freqs, 2, block, lanes)), (out,))


def solution(mesh):
    n_shot, n_rcv, halves = (mesh.shape[name] for name in ("shot", "rcv", "surf"))
    devices = mesh.devices.reshape(GROUPS, n_shot // GROUPS, n_rcv, halves)
    mesh = Mesh(devices, SHOT + ("rcv", "surf"))
    in_specs = (
        P("surf", SHOT, None),
        P("surf", SHOT, None),
        P("surf", SHOT),
        P("surf", SHOT),
        P(None, None, SHOT + ("surf",), "rcv"),
    )
    out_specs = P(None, None, SHOT + ("surf",), "rcv")
    return jax.shard_map(local, mesh=mesh, in_specs=in_specs, out_specs=out_specs, check_vma=False)
```

```python
import functools
import math

import jax
import jax.numpy as jnp
import numpy as np
from jax import lax
from jax.experimental import pallas as pl
from jax.experimental.pallas import tpu as pltpu
from jax.sharding import Mesh
from jax.sharding import PartitionSpec as P

SHOTS_PER_INDEX = 16
VMEM = pl.BlockSpec(memory_space=pltpu.VMEM)
LANES = 128
LIMIT = 16 * 1024 * 1024


GROUPS = 2
HEAD = 1
HEAD_COST, NEAR_COST, FAR_COST = 48, 24, 12
STACK = 7
SHOT = ("group", "member")


def share_of(group, member, members):
    return member ^ (group * (members // 2))


def dft_tables(window, members, n_rcv, halves, per, top):
    slots = -(-(2 * per + 4) // 16) * 16
    n = np.arange(window, dtype=np.int64)
    table = np.zeros((halves, n_rcv, members, slots, window), np.float64)
    share = per // halves
    for h, r, t in np.ndindex(halves, n_rcv, members):
        first = (t * n_rcv + r) * per
        freqs = [first + (h ^ k) * share + j for k in range(halves) for j in range(share)] + [top]
        for j, f in enumerate(freqs):
            angle = (n * f % window) * (2.0 * math.pi / window)
            table[h, r, t, 2 * j] = np.cos(angle)
            table[h, r, t, 2 * j + 1] = -np.sin(angle)
    table = table.reshape(halves * n_rcv, members, slots, window)
    table = (table / math.sqrt(window)).astype(np.float32)
    high = table.astype(jnp.bfloat16)
    low = (table - high.astype(np.float32)).astype(jnp.bfloat16)
    return jnp.asarray(high), jnp.asarray(low)


def nt(a, b):
    return lax.dot_general(a, b, (((1,), (1,)), ((), ())), preferred_element_type=jnp.float32)


def spectra_kernel(cols, x_ref, high_ref, low_ref, block_ref, shot_ref, point_ref, *out_refs):
    x = x_ref[...]
    mine = lax.axis_index("surf") * lax.axis_size("rcv") + lax.axis_index("rcv")
    first = share_of(lax.axis_index("group"), lax.axis_index("member"), high_ref.shape[1])
    slots = high_ref.shape[2]
    y = nt(jnp.concatenate([ref[mine, first ^ d] for ref in (high_ref, low_ref) for d in range(len(out_refs))], axis=0), x)
    y = y[: slots * len(out_refs)] + y[slots * len(out_refs) :]
    shot = (block_ref[...] * SHOTS_PER_INDEX + shot_ref[...]).astype(jnp.float32)
    point = point_ref[...].astype(jnp.float32)
    for d, out_ref in enumerate(out_refs):
        pieces = []
        for j in range(x.shape[0] // LANES):
            lanes = slice(j * LANES, (j + 1) * LANES)
            pieces += [y[d * slots : d * slots + cols + 2, lanes], shot[:, lanes], point[:, lanes]]
        out_ref[...] = jnp.concatenate(pieces, axis=0).astype(jnp.bfloat16)


def add_rows(cols, rows_ref, first_source, last_source, left_ref, acc_ref, low=0, high=None):
    high = cols + 3 if high is None else high
    chosen = (list(range(cols + 2)) + [None])[:high]
    _, shots, points = acc_ref.shape
    slots = cols + 4
    parts = rows_ref.shape[1] // slots
    group = lax.axis_index("group")

    def hits(source, count, slot, first):
        grid = lax.broadcasted_iota(jnp.int32, (count, LANES), 0).astype(jnp.float32)
        ids = [rows_ref[source, j * slots + slot : j * slots + slot + 1, :] for j in range(parts)]
        return [jnp.where(grid == i.astype(jnp.float32) - first, 1.0, 0.0).astype(jnp.bfloat16) for i in ids]

    def step(source, carry):
        shot_hit = hits(source, shots, cols + 2, 0.0)
        point_hit = jnp.concatenate(hits(source, points, cols + 3, (group * points).astype(jnp.float32)), axis=1)
        for first in range(low, high, STACK):
            stack = chosen[first : first + STACK]
            for i, slot in enumerate(stack):
                for j in range(parts):
                    left = shot_hit[j]
                    if slot is not None:
                        left = left * rows_ref[source, j * slots + slot : j * slots + slot + 1, :]
                    left_ref[i * shots : (i + 1) * shots, j * LANES : (j + 1) * LANES] = left
            got = nt(left_ref[: len(stack) * shots], point_hit)
            acc_ref[first : first + len(stack)] += got.reshape(len(stack), shots, points)
        return carry

    lax.fori_loop(first_source, last_source, step, 0)


def near_kernel(cols, first, last, rows_ref, *refs):
    *before, acc_ref, left_ref = refs
    acc_ref[...] = before[0][...] if before else jnp.zeros_like(acc_ref)
    add_rows(cols, rows_ref, first, last, left_ref, acc_ref)


def far_kernel(cols, outer_ref, inner_ref, near_ref, own_ref, panel_ref, scale_ref, all_ref, left_ref, acc_ref, pad_ref):
    each = cols // 2
    width = own_ref.shape[1]
    pad_ref[...] = jnp.zeros_like(pad_ref)
    pad_ref[:, pl.ds(pl.multiple_of(lax.axis_index("member") * width, width), width), :] = own_ref[...]
    acc_ref[...] = near_ref[...]
    all_ref[...] = outer_ref[...] + inner_ref[...]
    add_rows(cols, all_ref, 0, all_ref.shape[0], left_ref, acc_ref, low=each)
    scale = 1.0 / jnp.maximum(acc_ref[cols + 2], 1.0)
    scale_ref[...] = scale
    for c in range(each):
        panel_ref[c] = (acc_ref[each + c] * scale).astype(jnp.bfloat16)
    real = (acc_ref[cols] * scale).astype(jnp.bfloat16)
    imag = (acc_ref[cols + 1] * scale).astype(jnp.bfloat16)
    dot = functools.partial(jnp.dot, preferred_element_type=jnp.float32)
    panel_ref[each] = (dot(real, pad_ref[0]) - dot(imag, pad_ref[1])).astype(jnp.bfloat16)
    panel_ref[each + 1] = (dot(real, pad_ref[1]) + dot(imag, pad_ref[0])).astype(jnp.bfloat16)


def own_kernel(cols, all_ref, near_ref, sent_ref, scale_ref, panel_ref, left_ref, acc_ref):
    each = cols // 2
    acc_ref[:each] = near_ref[:each]
    add_rows(cols, all_ref, 0, all_ref.shape[0], left_ref, acc_ref, high=each)
    for c in range(each):
        panel_ref[c] = (acc_ref[c] * scale_ref[...]).astype(jnp.bfloat16)
    panel_ref[each:] = sent_ref[each:]


def product_kernel(members, n_shot, n_rcv, halves, width, *refs):
    panel_refs, (recv_ref, out_ref) = refs[:halves], refs[halves:]
    per, shots, points = panel_refs[0].shape[0] // 2 - 1, panel_refs[0].shape[1], panel_refs[0].shape[2]
    lanes = recv_ref.shape[2]
    block = shots // (n_shot * halves)
    own_half, mine = lax.axis_index("surf"), lax.axis_index("rcv")
    for f in range(per):
        left = [ref[2 * f : 2 * f + 2].reshape(2 * shots, points) for ref in panel_refs]
        left = jnp.concatenate(left, axis=1)
        sides = []
        for c in range(2):
            first = (2 * f + c) * width
            blocks = [
                jnp.concatenate(
                    [
                        recv_ref[(t * n_rcv + r) * halves + (own_half ^ k), first : first + width, :]
                        for k in range(halves)
                        for t in range(members)
                    ],
                    axis=0,
                )
                for r in range(n_rcv)
            ]
            right = blocks[0] if n_rcv == 1 else jnp.concatenate(blocks, axis=1)
            sides.append(jnp.dot(left, right, preferred_element_type=jnp.float32))
        real = sides[0][:shots] - sides[1][shots:]
        imag = sides[1][:shots] + sides[0][shots:]
        for s in range(n_shot):
            for h in range(halves):
                first = (s * halves + h) * block
                both = jnp.concatenate([real[first : first + block], imag[first : first + block]], axis=0)
                for r in range(n_rcv):
                    part = both[:, r * lanes : (r + 1) * lanes].astype(jnp.bfloat16)
                    out_ref[(s * n_rcv + r) * halves + h, 2 * f * block : 2 * (f + 1) * block, :] = part
    top = panel_refs[0][2 * per + own_half].astype(jnp.float32)
    for ref in panel_refs[1:]:
        top = top + ref[2 * per + own_half].astype(jnp.float32)
    for r in range(n_rcv):
        part = jnp.where(mine == r, top, jnp.zeros_like(top)).astype(jnp.bfloat16)
        for s in range(n_shot):
            for h in range(halves):
                first = (s * halves + h) * block
                out_ref[(s * n_rcv + r) * halves + h, 2 * per * block :, :] = part[first : first + block]


def gather_kernel(per, groups, halves, got_ref, out_ref):
    block = out_ref.shape[2]
    each = got_ref.shape[0] // groups
    rows = 2 * per * block
    tops = [jnp.zeros((block, got_ref.shape[2]), jnp.float32) for _ in range(halves)]
    for w in range(each):
        value = jnp.zeros((rows, got_ref.shape[2]), jnp.float32)
        for g in range(groups):
            source = g * each + share_of(g, w, each)
            value = value + got_ref[source, :rows, :].astype(jnp.float32)
            tops[w % halves] = tops[w % halves] + got_ref[source, rows:, :].astype(jnp.float32)
        out_ref[w * per : (w + 1) * per] = value.reshape((per,) + out_ref.shape[1:]).astype(jnp.bfloat16)
    for c in range(halves):
        out_ref[each * per, c] = tops[c].astype(jnp.bfloat16)


def call(kernel, out_shape, operands, scratch=(), limit=LIMIT, flops=None):
    return pl.pallas_call(
        kernel,
        out_shape=out_shape,
        in_specs=[VMEM] * len(operands),
        out_specs=jax.tree.map(lambda _: VMEM, out_shape),
        scratch_shapes=list(scratch),
        compiler_params=pltpu.CompilerParams(vmem_limit_bytes=limit),
        cost_estimate=flops and pl.CostEstimate(flops=flops, transcendentals=0, bytes_accessed=0),
    )(*operands)


def local(traces, trace_block, trace_shot, trace_point, recv_panel):
    groups, members = lax.axis_size("group"), lax.axis_size("member")
    n_shot, n_rcv, halves = groups * members, lax.axis_size("rcv"), lax.axis_size("surf")
    freqs, _, width, lanes = recv_panel.shape
    window, n_rows = traces.shape[2], traces.shape[1]
    shots, points = SHOTS_PER_INDEX * n_shot, width * members
    assert max(shots, points * groups) <= 256
    main = freqs - 1
    owners = members * n_rcv * halves
    per = main // owners
    assert per * owners == main and halves == 2 and points == lanes
    cols = 2 * per * halves
    block = shots // (n_shot * halves)
    bf16 = functools.partial(jax.ShapeDtypeStruct, dtype=jnp.bfloat16)
    high, low = dft_tables(window, members, n_rcv, halves, per * halves, main)

    message = bf16((n_rows // LANES * (cols + 4), LANES))
    messages = call(
        functools.partial(spectra_kernel, cols),
        (message,) * members,
        (traces[0], high, low, trace_block.reshape(1, n_rows), trace_shot, trace_point),
        limit=56 * 1024 * 1024,
    )
    near = [messages[0]]
    for d in range(members - 1, 0, -1):
        near.append(lax.ppermute(messages[d], "member", [(t, t ^ d) for t in range(members)]))
    near = jnp.stack(near)
    pairs = [(m, members + share_of(1, m, members)) for m in range(members)]
    outer, inner = (chosen + [(b, a) for a, b in chosen] for chosen in (pairs[: members // 2], pairs[members // 2 :]))
    outer = lax.ppermute(near, SHOT, outer)

    share = main // 2
    swap = lax.axis_index("group") * share
    recv = [lax.dynamic_slice_in_dim(recv_panel, start, share, 0) for start in (swap, share - swap)]
    recv = jnp.concatenate(recv, axis=0).reshape(owners, per * 2 * width, lanes)
    recv, near = lax.optimization_barrier((recv, near))
    recv = lax.all_to_all(recv, ("member", "rcv", "surf"), split_axis=0, concat_axis=0, tiled=True)

    acc = jax.ShapeDtypeStruct((cols + 3, shots, points), jnp.float32)
    left = pltpu.VMEM((STACK * shots, n_rows), jnp.bfloat16)
    work = (cols + 3) * shots * points * n_rows
    acc_near = call(functools.partial(near_kernel, cols, 0, HEAD), acc, (near,), (left,), flops=HEAD_COST * work)
    tied, acc_near = lax.optimization_barrier((near, acc_near))
    inner = lax.ppermute(tied, SHOT, inner)
    acc_near = call(functools.partial(near_kernel, cols, HEAD, members), acc, (near, acc_near), (left,), flops=NEAR_COST * work)
    panel = bf16((2 * per + 2, shots, points))
    scratch = (left, pltpu.VMEM(acc.shape, jnp.float32))
    sent, scale, every = call(
        functools.partial(far_kernel, cols),
        (panel, jax.ShapeDtypeStruct((shots, points), jnp.float32), bf16(near.shape)),
        (outer, inner, acc_near, recv_panel[main]),
        scratch + (pltpu.VMEM((2, points, lanes), jnp.bfloat16),),
        flops=FAR_COST * work,
    )
    came = lax.ppermute(sent, "surf", [(h, h ^ 1) for h in range(halves)])
    own = call(functools.partial(own_kernel, cols), panel, (every, acc_near, sent, scale), scratch, flops=FAR_COST * work)
    panels = [own, came]
    out = call(
        functools.partial(product_kernel, members, n_shot, n_rcv, halves, width),
        bf16((n_shot * n_rcv * halves, (2 * per + 1) * block, lanes)),
        (*panels, recv),
    )
    out = lax.all_to_all(out, SHOT + ("rcv", "surf"), split_axis=0, concat_axis=0, tiled=True)
    return call(functools.partial(gather_kernel, per, groups, halves), bf16((freqs, 2, block, lanes)), (out,))


def solution(mesh):
    n_shot, n_rcv, halves = (mesh.shape[name] for name in ("shot", "rcv", "surf"))
    devices = mesh.devices.reshape(GROUPS, n_shot // GROUPS, n_rcv, halves)
    mesh = Mesh(devices, SHOT + ("rcv", "surf"))
    in_specs = (
        P("surf", SHOT, None),
        P("surf", SHOT, None),
        P("surf", SHOT),
        P("surf", SHOT),
        P(None, None, SHOT + ("surf",), "rcv"),
    )
    out_specs = P(None, None, SHOT + ("surf",), "rcv")
    return jax.shard_map(local, mesh=mesh, in_specs=in_specs, out_specs=out_specs, check_vma=False)
```
